32 devices in a mesh: lon: 8 (over y, x, core), lat: 4 (over z).
Axes of the slice: x: 2, y: 2, z: 4, core: 2. Of those that a mesh axis runs over, the one named last changes fastest.
Arguments:
- fields: bfloat16 [2, 96, 192, 512], P(None, 'lat', 'lon'), may hold values from -6 to 6
- cotangent: bfloat16 [2, 96, 192, 512], P(None, 'lat', 'lon'), may hold values from -6 to 6
- qkv_weight: bfloat16 [512, 1536], replicated, may hold values from -1 to 1, as said below
- out_weight: bfloat16 [512, 512], replicated, may hold values from -0.25 to 0.25
Outputs:
- output_field: bfloat16 [2, 96, 192, 512], P(None, 'lat', 'lon')
- field_grad: bfloat16 [2, 96, 192, 512], P(None, 'lat', 'lon')
- qkv_grad: float32 [512, 1536], P(('lon', 'lat'))
- out_grad: float32 [512, 512], P(('lon', 'lat'))
The draws below stay inside these ranges and needn't reach their ends.
Inputs may be any that keep to these rules, and one draw needn't show every extreme that they name: `qkv_weight`: a dense projection matrix, about 512^-0.5 in scale.
All inputs are finite; a program needn't handle non-finite values.
Results may differ from the reference program's by a relative error of at most 0.015.
Values may be sent and summed in bfloat16 or wider, within the bound.
No kernel may reach another device: no remote copies, remote signals or barrier semaphores. Data moves between devices by JAX's collectives and lax.ppermute only.
A program may use at most 192 MiB of HBM per device.

```python
import jax
import jax.numpy as jnp
from jax import lax

D = 512
HEADS = 16
LV = 2
WIN_LAT = 6
WIN_LON = 12
NLAT = 96
NLON = 192


def draw_qkv_weight(key, part):
    key = jax.random.fold_in(key, 11)
    base = jnp.clip(jax.random.normal(key, (D, 3 * D), jnp.float32), -4.0, 4.0)
    return (base * D ** (-0.5)).astype(jnp.bfloat16)


def spiked(array, own_key, source, target, blocks, factor):
    def block_of(dim):
        return (jnp.arange(array.shape[dim]) // (array.shape[dim] // blocks)).reshape((-1,) + (1,) * (array.ndim - 1 - dim))

    first = jax.random.permutation(own_key, blocks)[block_of(target)]
    second = (block_of(target) + blocks // 2) % blocks
    return jnp.where((block_of(source) == first) | (block_of(source) == second), factor * array, array)


def steps_of(own_key, dims, pieces, low, top_value):
    def one(position, parts):
        draws = jax.random.uniform(jax.random.fold_in(jax.random.fold_in(own_key, 6), position), (parts,), jnp.float32, low / len(pieces), top_value / len(pieces))
        return jnp.repeat(jnp.exp(draws), dims[position] // parts).reshape((-1,) + (1,) * (len(dims) - position - 1))

    loudness = one(*pieces[0])
    for cut in pieces[1:]:
        loudness = loudness * one(*cut)
    return loudness


def normal_values(key, shape, scale, reach, split=(), held_as=jnp.bfloat16):
    loudness = steps_of(key, shape, split, -0.22, 0.18) if split else 1.0
    entries = jax.random.normal(key, shape, jnp.float32) * scale * loudness
    return jnp.minimum(jnp.maximum(entries, -reach), reach).astype(held_as)


def noise_with(key, shape, scale, limit, cuts, heavy, kind=jnp.bfloat16):
    values = scale * jax.random.normal(key, shape, jnp.float32)
    if cuts:
        values = values * steps_of(key, shape, cuts, -0.22, 0.18)
    return jnp.clip(spiked(values, jax.random.fold_in(key, 3), *heavy), -limit, limit).astype(kind)


def setup_inputs(seed: int = 0) -> dict:
    keys = jax.random.split(jax.random.key(seed), 5)
    fields = noise_with(keys[0], (LV, NLAT, NLON, D), 1.0, 6.0, ((1, 4), (2, 8)), (2, 3, 8, 2.0))
    cotangent = normal_values(keys[1], (LV, NLAT, NLON, D), 1.0, 6.0, ((1, 4), (2, 8)))
    qkv_weight = draw_qkv_weight(jax.random.fold_in(keys[4], 71), 0)
    out_weight = normal_values(keys[3], (D, D), D ** -0.5, 0.25)
    return dict(fields=fields, cotangent=cotangent, qkv_weight=qkv_weight, out_weight=out_weight)


def normalize(values):
    center = lax.optimization_barrier(jnp.mean(values, axis=-1, keepdims=True))
    centred = values - center
    spread = lax.optimization_barrier(jnp.mean(centred * centred, axis=-1, keepdims=True))
    return centred * lax.rsqrt(spread + 1e-05)

def attend(projected, groups):
    wincount, tokens_win, triple = projected.shape
    width = triple // 3
    head_size = width // HEADS
    queries = projected[..., :width].reshape(wincount, tokens_win, HEADS, head_size).astype(jnp.float32)
    keyset = projected[..., width:2 * width].reshape(wincount, tokens_win, HEADS, head_size).astype(jnp.float32)
    valueset = projected[..., 2 * width:].reshape(wincount, tokens_win, HEADS, head_size).astype(jnp.float32)
    scores = jnp.einsum('wqhe,wkhe->whqk', queries, keyset) * head_size ** (-0.5)
    allowed = (groups[:, :, None] == groups[:, None, :])[:, None]
    scores = jnp.where(allowed, scores, -1000000000.0)
    highest = lax.optimization_barrier(jnp.max(scores, axis=-1, keepdims=True))
    raised = jnp.exp(scores - highest)
    soft_weights = (raised / lax.optimization_barrier(jnp.sum(raised, axis=-1, keepdims=True))).astype(jnp.bfloat16)
    mixture = jnp.einsum('whqk,wkhe->wqhe', soft_weights.astype(jnp.float32), valueset)
    return mixture.reshape(wincount, tokens_win, width).astype(jnp.bfloat16)

def to_windows(grid):
    levels, lat_cells, lon_cells, channels = grid.shape
    shaped = grid.reshape(levels, lat_cells // WIN_LAT, WIN_LAT, lon_cells // WIN_LON, WIN_LON, channels)
    shaped = shaped.transpose(1, 3, 0, 2, 4, 5)
    return shaped.reshape(lat_cells // WIN_LAT * (lon_cells // WIN_LON), levels * WIN_LAT * WIN_LON, channels)

def from_windows(windows, levels, lat_cells, lon_cells):
    channels = windows.shape[-1]
    shaped = windows.reshape(lat_cells // WIN_LAT, lon_cells // WIN_LON, levels, WIN_LAT, WIN_LON, channels)
    shaped = shaped.transpose(2, 0, 3, 1, 4, 5)
    return shaped.reshape(levels, lat_cells, lon_cells, channels)

def reference(fields, cotangent, qkv_weight, out_weight):
    shift_lat = WIN_LAT // 2
    shift_lon = WIN_LON // 2
    rolled = jnp.roll(fields, (-shift_lat, -shift_lon), axis=(1, 2))
    windows = to_windows(rolled)
    wincount, tokens_win, width = windows.shape
    tokens_flat = windows.reshape(-1, width)
    lat_rows = jnp.arange(NLAT, dtype=jnp.int32)
    group_rows = (lat_rows >= NLAT - shift_lat).astype(jnp.int32)
    group_grid = jnp.broadcast_to(group_rows[None, :, None, None], (LV, NLAT, NLON, 1)).astype(jnp.int32)
    groups = to_windows(group_grid)[..., 0]
    norm_core, norm_back = jax.vjp(normalize, tokens_flat.astype(jnp.float32))
    normed = norm_core.astype(jnp.bfloat16)
    projected = jnp.dot(normed, qkv_weight, preferred_element_type=jnp.float32).astype(jnp.bfloat16)
    row_windows = NLON // WIN_LON

    def attend_all(values):
        shaped = values.reshape(wincount // row_windows, row_windows, tokens_win, 3 * width)
        shaped_groups = groups.reshape(wincount // row_windows, row_windows, tokens_win)
        result = lax.map(lambda operands: attend(operands[0], operands[1]), (shaped, shaped_groups))
        return result.reshape(wincount, tokens_win, width)
    mixture, attend_back = jax.vjp(attend_all, projected.reshape(wincount, tokens_win, 3 * width))
    attended = mixture.reshape(-1, width)
    output_rows = (tokens_flat.astype(jnp.float32) + jnp.dot(attended, out_weight, preferred_element_type=jnp.float32)).astype(jnp.bfloat16)
    output_grid = from_windows(output_rows.reshape(wincount, tokens_win, width), LV, NLAT, NLON)
    output_field = jnp.roll(output_grid, (shift_lat, shift_lon), axis=(1, 2))
    grad_rolled = jnp.roll(cotangent, (-shift_lat, -shift_lon), axis=(1, 2))
    grad_rows = to_windows(grad_rolled).reshape(-1, width)
    out_grad = lax.dot_general(attended, grad_rows, (((0,), (0,)), ((), ())), preferred_element_type=jnp.float32)
    grad_attended = lax.dot_general(grad_rows, out_weight, (((1,), (1,)), ((), ())), preferred_element_type=jnp.float32).astype(jnp.bfloat16)
    grad_projected = attend_back(grad_attended.reshape(wincount, tokens_win, width))[0].reshape(-1, 3 * width)
    qkv_grad = lax.dot_general(normed, grad_projected, (((0,), (0,)), ((), ())), preferred_element_type=jnp.float32)
    grad_normed = lax.dot_general(grad_projected, qkv_weight, (((1,), (1,)), ((), ())), preferred_element_type=jnp.float32)
    grad_centred = norm_back(grad_normed)[0]
    grad_tokens = (grad_rows.astype(jnp.float32) + grad_centred).astype(jnp.bfloat16)
    grad_grid = from_windows(grad_tokens.reshape(wincount, tokens_win, width), LV, NLAT, NLON)
    field_grad = jnp.roll(grad_grid, (shift_lat, shift_lon), axis=(1, 2))
    return (output_field, field_grad, qkv_grad, out_grad)
```

```python
import functools

import jax
import jax.numpy as jnp
from jax import lax
from jax.experimental import pallas as pl
from jax.experimental.pallas import tpu as pltpu
from jax.sharding import PartitionSpec as P

HEADS = 16
WIN_LAT = 6
WIN_LON = 12
TOKENS = 144
MAIN = 128
TAIL = TOKENS - MAIN
GROUP = 8
F32 = jnp.float32
BF16 = jnp.bfloat16
VMEM_LIMIT = 36 * 1024 * 1024


def nn(a, b):
    return lax.dot_general(a, b, (((1,), (0,)), ((), ())), preferred_element_type=F32)


def nt(a, b):
    return lax.dot_general(a, b, (((1,), (1,)), ((), ())), preferred_element_type=F32)


def sublane(shape):
    return lax.broadcasted_iota(jnp.int32, shape, len(shape) - 2)


def inner_lanes(shape):
    sub = sublane(shape)
    return (sub >= 2) & (sub < 6)


def first_window(a, b, c):
    width = b.shape[-1]
    edge = jnp.where(sublane(a.shape) >= 6, a, c)
    inner = inner_lanes((6,) + a.shape[1:])
    mixed = jnp.where(inner, jnp.roll(edge[6:], 4, axis=1), edge[:6])
    return jnp.concatenate([b.reshape(96, width), mixed.reshape(48, width)], axis=0)


def second_window(a, c):
    width = a.shape[-1]
    late = jnp.where(sublane(a.shape) < 6, a, c)
    inner = inner_lanes((6,) + a.shape[1:])
    mixed = jnp.where(inner, c[:6], jnp.roll(c[6:], 4, axis=1))
    return jnp.concatenate([late.reshape(96, width), mixed.reshape(48, width)], axis=0)


def windows_to_band(w0, w1):
    width = w0.shape[-1]
    b = w0[:96].reshape(12, 8, width)
    late = w1[:96].reshape(12, 8, width)
    first = w0[96:].reshape(6, 8, width)
    second = w1[96:].reshape(6, 8, width)
    edge = jnp.concatenate([first, jnp.roll(first, 4, axis=1)], axis=0)
    mid = jnp.concatenate([second, jnp.roll(second, 4, axis=1)], axis=0)
    sub = sublane(b.shape)
    a = jnp.where(sub < 6, late, edge)
    c = jnp.where(sub < 2, edge, jnp.where(sub < 6, mid, late))
    return a, b, c


def statistics(x):
    center = jnp.mean(x, axis=-1, keepdims=True)
    centred = x - center
    spread = jnp.mean(centred * centred, axis=-1, keepdims=True)
    return centred, lax.rsqrt(spread + 1e-05)


class Copies:
    def __init__(self, sems):
        self.sems = sems
        self.used = 0

    def start(self, source, target):
        copy = pltpu.make_async_copy(source, target, self.sems.at[self.used])
        self.used += 1
        copy.start()
        return copy


def pack_edges(sets):
    last = sets[3].astype(F32)
    whole = sublane(last.shape) < 6
    return [
        jnp.where(whole, sets[k].astype(F32), jnp.roll(last, 6 - 2 * k, axis=1)).astype(BF16)
        for k in range(3)
    ]


def edge_rows(lon_ref, arr, level, start, size):
    parts = [lon_ref[k, start : start + size].astype(F32) for k in range(3)]
    if 2 * arr + level < 3:
        return parts[2 * arr + level]
    sub = sublane(parts[0].shape)
    late = jnp.where(sub < 4, jnp.roll(parts[1], 4, axis=1), jnp.roll(parts[2], 6, axis=1))
    return jnp.where(sub < 2, jnp.roll(parts[0], 2, axis=1), late)


def pack_kernel(f_hbm, c_hbm, lat_ref, lon_ref, cor_ref, edge_ref, sems):
    copies = Copies(sems)
    waits = []
    for arr, hbm in enumerate((f_hbm, c_hbm)):
        waits.append(copies.start(hbm.at[:, 3:, :16], edge_ref.at[arr]))
        waits.append(copies.start(hbm.at[:, :3], lat_ref.at[arr]))
    for wait in waits:
        wait.wait()
    cor_ref[...] = lat_ref[:, :, :, :8]
    sets = [edge_ref[k // 2, k % 2, :, :8] for k in range(4)]
    for k, packed in enumerate(pack_edges(sets)):
        lon_ref[k] = packed


def own_band(src, start):
    planes = [src[level, start : start + WIN_LAT].astype(F32) for level in range(2)]
    x = jnp.concatenate(planes, axis=0)
    return x[:, 0:8], x[:, 8:16], x[:, 16:24]


def with_neighbours(src, lat_ref, lon_ref, cor_ref, arr, band):
    start = 3 + band * WIN_LAT
    rows = src.shape[1]
    planes, edges = [], []
    for level in range(2):
        if start + WIN_LAT <= rows:
            planes.append(src[level, start : start + WIN_LAT])
            edges.append(edge_rows(lon_ref, arr, level, start - 3, WIN_LAT))
        else:
            planes.extend([src[level, start:], lat_ref[arr, level]])
            edges.extend([edge_rows(lon_ref, arr, level, start - 3, 3), cor_ref[arr, level]])
    x = jnp.concatenate([p.astype(F32) for p in planes], axis=0)
    edge = jnp.concatenate([e.astype(F32) for e in edges], axis=0)
    a = jnp.where(sublane(edge.shape) < 6, edge, x[:, 0:8])
    return a, x[:, 8:16], x[:, 16:24]


def store_window(arr, values, place, x_ref, n_ref, g_ref):
    if arr == 0:
        x_ref[place] = values.astype(BF16)
        centred, scale = statistics(values)
        n_ref[place] = (centred * scale).astype(BF16)
    else:
        g_ref[place] = values.astype(BF16)


def extend(x):
    return jnp.concatenate([x[:MAIN]] + [x[MAIN:]] * GROUP, axis=0)


def tail_mask():
    rows = lax.broadcasted_iota(jnp.int32, (256, 128), 0) // 32
    lanes = lax.broadcasted_iota(jnp.int32, (256, 128), 1) // TAIL
    return rows == lanes


def head_tile(block, head):
    parts = []
    if head > 0:
        parts.append(jnp.zeros((32 * head, 128), block.dtype))
    parts.append(block)
    if head < GROUP - 1:
        parts.append(jnp.zeros((32 * (GROUP - 1 - head), 128), block.dtype))
    return jnp.concatenate(parts, axis=0)


def window_attention(normed, grads, natural_kv, wt, wo, bias, fold, att_ref, dp_ref):
    head_size = 32
    scale = head_size ** (-0.5)
    factor = scale * 1.4426950408889634
    mask = tail_mask()
    groups = range(2)
    turned = nt(wt, extend(normed)).astype(BF16)
    turned_grads = nt(wo, extend(grads))
    turned_kv = natural_kv.T
    keys = [natural_kv[:, 256 * g : 256 * g + 256] for g in groups]
    values = [natural_kv[:, 512 + 256 * g : 768 + 256 * g] for g in groups]
    kt = [turned_kv[256 * g : 256 * g + 256] for g in groups]
    vt = [turned_kv[512 + 256 * g : 768 + 256 * g] for g in groups]
    dot = [turned_grads[256 * g : 256 * g + 256] for g in groups]

    def tiles_of(main, tail):
        tiles = []
        for j in range(GROUP // 2):
            tiles.append(
                jnp.concatenate(
                    [head_tile(main[32 * h : 32 * h + 32], h) for h in (2 * j, 2 * j + 1)], axis=1
                )
            )
        return tiles + [tail]

    q_tiles = []
    for g in groups:
        part = turned[256 * g : 256 * g + 256]
        q_tiles.append(tiles_of(part[:, :128], jnp.where(mask, part[:, 128:], jnp.zeros((), BF16))))
    yield
    order = [(j, g) for j in range(GROUP // 2 + 1) for g in groups]
    ahead = 2

    def channels(rows, tile, j):
        if j == GROUP // 2:
            return nn(rows, tile)
        first = 128 * (j // 2)
        return nn(rows[:, first : first + 128], tile[first : first + 128])

    def score(j, g):
        scores = channels(keys[g], q_tiles[g][j], j)
        if bias is None:
            return scores
        part = bias[:, :128] if j < 4 else bias[:, 128:]
        return scores + (jnp.concatenate([part, part], axis=1) if j < 4 else part)

    soft = [[], []]
    inverse = [[], []]
    mixed = [[], []]
    waiting = [score(*at) for at in order[:ahead]]
    for i, (j, g) in enumerate(order):
        if i + ahead < len(order):
            waiting.append(score(*order[i + ahead]))
        scores = waiting[i]
        raised = jnp.exp2((scores - jnp.max(scores, axis=0, keepdims=True)) * factor)
        inv = 1.0 / jnp.sum(raised, axis=0, keepdims=True)
        held = raised.astype(BF16)
        soft[g].append(held)
        inverse[g].append(inv)
        if j < 4:
            out = nn(vt[g][64 * j : 64 * j + 64], held)
            mixed[g].append(out[:32, :128] * inv[:, :128])
            mixed[g].append(out[32:, 128:] * inv[:, 128:])
        else:
            out = nn(vt[g], held)
            mixed[g].append(jnp.where(mask, out * inv, 0.0))
        yield
    do_tiles = [None, None]
    deltas = [None, None]
    for g in groups:
        scaled, sums = [], []
        for h in range(GROUP):
            inv = inverse[g][h // 2][:, 128 * (h % 2) : 128 * (h % 2) + 128]
            scaled.append((dot[g][32 * h : 32 * h + 32, :128] * inv).astype(BF16))
            sums.append(jnp.sum(scaled[h].astype(F32) * mixed[g][h], axis=0, keepdims=True))
        tail = jnp.where(mask, dot[g][:, 128:] * inverse[g][4], 0.0).astype(BF16)
        deltas[g] = [jnp.concatenate(sums[2 * j : 2 * j + 2], axis=1) for j in range(GROUP // 2)]
        deltas[g].append(jnp.sum(tail.astype(F32) * mixed[g][GROUP], axis=0, keepdims=True))
        do_tiles[g] = tiles_of(jnp.concatenate(scaled, axis=0), tail)
        yield
    slopes = [[], []]
    dq = [[], []]
    waiting = [channels(values[g], do_tiles[g][j], j) for j, g in order[:ahead]]
    for i, (j, g) in enumerate(order):
        if i + ahead < len(order):
            k, f = order[i + ahead]
            waiting.append(channels(values[f], do_tiles[f][k], k))
        slope = (soft[g][j].astype(F32) * (waiting[i] - deltas[g][j])).astype(BF16)
        slopes[g].append(slope)
        if j < 4:
            out = nn(kt[g][64 * j : 64 * j + 64], slope) * scale
            dq[g].append(out[:32, :128])
            dq[g].append(out[32:, 128:])
        else:
            out = nn(kt[g], slope) * scale
            dq[g].append(jnp.where(mask, out, 0.0))
        yield
    def by_keys(rows, tiles):
        halves = []
        for i in range(2):
            part = slice(128 * i, 128 * i + 128)
            pair = (2 * i, 2 * i + 1)
            halves.append(
                nt(
                    jnp.concatenate([rows[j] for j in pair], axis=1),
                    jnp.concatenate([tiles[j][part] for j in pair], axis=1),
                )
            )
        return jnp.concatenate(halves, axis=1) + nt(rows[GROUP // 2], tiles[GROUP // 2])

    def natural(blocks):
        main = jnp.concatenate(blocks[:GROUP], axis=0)
        tail = nt(fold, blocks[GROUP].astype(BF16))
        return jnp.concatenate([main.T, tail], axis=0)

    for g in groups:
        span = slice(256 * g, 256 * g + 256)
        att_ref[:, span] = natural(mixed[g]).astype(BF16)
        yield
        dv = by_keys(soft[g], do_tiles[g])
        dp_ref[:, 1024 + 256 * g : 1280 + 256 * g] = dv.astype(BF16)
        yield
        dk = by_keys(slopes[g], q_tiles[g]) * scale
        dp_ref[:, 512 + 256 * g : 768 + 256 * g] = dk.astype(BF16)
        yield
        dp_ref[:, span] = natural(dq[g]).astype(BF16)
        yield


FORWARD = 12


def in_turns(windows):
    waiting, active, done = list(windows), [], {}
    while waiting or active:
        if waiting and (not active or (len(active) < 3 and done[active[-1][0]] >= FORWARD)):
            number = len(windows) - len(waiting)
            active.append((number, waiting.pop(0)))
            done[number] = 0
        for item in list(active):
            try:
                next(item[1])
                done[item[0]] += 1
            except StopIteration:
                active.remove(item)


def fill_bias(bias_ref, last):
    def row_of(token):
        return jnp.where(token < 96, (token // 8) % 6, (token - 96) // 8) >= 3

    keys = row_of(lax.broadcasted_iota(jnp.int32, (TOKENS, 256), 0))
    lane = lax.broadcasted_iota(jnp.int32, (TOKENS, 256), 1)
    queries = row_of(jnp.where(lane < MAIN, lane, MAIN + lane % TAIL))
    bias_ref[...] = jnp.where((keys != queries) & (last == 1), -1e10, 0.0)


def split_rows(total_ref, core, mine_ref, send_ref):
    count, rows = mine_ref.shape[0], mine_ref.shape[1]
    for i in range(count):
        mine_ref[i] = total_ref[pl.ds((2 * i + core) * rows, rows)]
        send_ref[i] = total_ref[pl.ds((2 * i + 1 - core) * rows, rows)]


def fold_matrix():
    lanes = lax.broadcasted_iota(jnp.int32, (TAIL, 128), 1) % TAIL
    return (lanes == lax.broadcasted_iota(jnp.int32, (TAIL, 128), 0)).astype(BF16)


def flat(ref):
    return ref[...].reshape(-1, ref.shape[-1])


def back_of_windows(x_ref, g_ref, att_ref, dp_ref, w, wo):
    mixture = nn(flat(att_ref), wo)
    grads = nt(flat(dp_ref), w)
    pairs = []
    for i in range(x_ref.shape[0]):
        rows = slice(TOKENS * i, TOKENS * i + TOKENS)
        x, grad = x_ref[i].astype(F32), grads[rows]
        centred, scale = statistics(x)
        hat = centred * scale
        back = grad - jnp.mean(grad, axis=-1, keepdims=True)
        back = back - hat * jnp.mean(grad * hat, axis=-1, keepdims=True)
        tokens = g_ref[i].astype(F32) + back * scale
        pairs.append(((x + mixture[rows]).astype(BF16), tokens.astype(BF16)))
    return pairs


def inner_kernel(f_hbm, c_hbm, w_ref, wo_ref, *refs):
    outs, (f_ref, c_ref, x_ref, kv_ref, wt_ref, sems), results = refs[:6], refs[6:12], refs[12:]
    n_ref, g_ref, att_ref, dp_ref, out_ref, grad_ref = results
    copies = Copies(sems)
    count = n_ref.shape[0]
    rows = [pl.ds(3 + band * WIN_LAT, WIN_LAT) for band in range(count)]
    got = [
        [copies.start(hbm.at[:, rows[band]], ref.at[band]) for band in range(count)]
        for hbm, ref in ((f_hbm, f_ref), (c_hbm, c_ref))
    ]

    def front(arr, src):
        for band in range(count):
            got[arr][band].wait()
            store_window(arr, first_window(*own_band(src[band], 0)), band, x_ref, n_ref, g_ref)

    wt_ref[...] = w_ref[:, :512].T
    front(0, f_ref)
    kv_ref[...] = nn(flat(n_ref), w_ref[:, 512:]).astype(BF16).reshape(kv_ref.shape)
    front(1, c_ref)
    sent = [copies.start(results[k], outs[k]) for k in range(2)]
    fold = fold_matrix()

    in_turns(
        [
            window_attention(
                n_ref[i],
                g_ref[i],
                kv_ref[i],
                wt_ref[...],
                wo_ref[...],
                None,
                fold,
                att_ref.at[i],
                dp_ref.at[i],
            )
            for i in range(count)
        ]
    )
    sent += [copies.start(results[k], outs[k]) for k in (2, 3)]
    pairs = back_of_windows(x_ref, g_ref, att_ref, dp_ref, w_ref[...], wo_ref[...])
    for i, (out, grad) in enumerate(pairs):
        out_ref[i] = out
        grad_ref[i] = grad
        sent += [copies.start(results[k].at[i], outs[k].at[i]) for k in (4, 5)]
    for copy in sent:
        copy.wait()


def outer_kernel(where_ref, f_hbm, c_hbm, lat_ref, lon_ref, cor_ref, w_ref, wo_hbm, *refs):
    ins, refs = refs[:4], refs[4:]
    x_ref, g_ref, att_ref, dp_ref, mine_ref, send_ref, f_ref, c_ref = refs[:8]
    held, (wo_ref, n_ref, kv_ref, wt_ref, bias_ref, total_ref, sems) = refs[8:12], refs[12:]
    copies = Copies(sems)
    count = n_ref.shape[0]
    bands = count - 1
    spans = []
    for band in range(bands):
        start = 3 + band * WIN_LAT
        spans.append(pl.ds(start, min(WIN_LAT, f_ref.shape[1] - start)))
    got = [
        [copies.start(hbm.at[:, span], ref.at[:, span]) for span in spans]
        for hbm, ref in ((f_hbm, f_ref), (c_hbm, c_ref))
    ]
    wo_copy = copies.start(wo_hbm, wo_ref)
    terms = [copies.start(*pair) for pair in zip(ins, held)]

    def front(arr, src):
        for band in range(bands):
            got[arr][band].wait()
            a, b, c = with_neighbours(src, lat_ref, lon_ref, cor_ref, arr, band)
            store_window(arr, second_window(a, c), band, x_ref, n_ref, g_ref)
            if band == bands - 1:
                store_window(arr, first_window(a, b, c), band + 1, x_ref, n_ref, g_ref)

    wt_ref[...] = w_ref[:, :512].T
    fill_bias(bias_ref, where_ref[0])
    front(0, f_ref)
    kv_ref[...] = nn(flat(n_ref), w_ref[:, 512:]).astype(BF16).reshape(kv_ref.shape)
    front(1, c_ref)
    fold = fold_matrix()

    wo_copy.wait()
    in_turns(
        [
            window_attention(
                n_ref[i],
                g_ref[i],
                kv_ref[i],
                wt_ref[...],
                wo_ref[...],
                bias_ref[...] if i >= bands - 1 else None,
                fold,
                att_ref.at[i],
                dp_ref.at[i],
            )
            for i in range(count)
        ]
    )
    for copy in terms:
        copy.wait()
    inner_n, inner_g, inner_att, inner_dp = held
    total_ref[:, :1536] = (
        nn(flat(n_ref).T, flat(dp_ref)) + nn(flat(inner_n).T, flat(inner_dp))
    ).astype(BF16)
    total_ref[:, 1536:] = (
        nn(flat(att_ref).T, flat(g_ref)) + nn(flat(inner_att).T, flat(inner_g))
    ).astype(BF16)
    split_rows(total_ref, where_ref[1], mine_ref, send_ref)


def outer_back_kernel(x_ref, g_ref, att_ref, dp_ref, w_ref, wo_ref, *refs):
    outs, (lat_out, lon_out), results, sems = refs[:2], refs[2:4], refs[4:6], refs[6]
    copies = Copies(sems)
    count = x_ref.shape[0]
    bands = count - 1
    sent = []
    pairs = back_of_windows(x_ref, g_ref, att_ref, dp_ref, w_ref[...], wo_ref[...])
    for i, pair in enumerate(pairs):
        for values, ref, hbm in zip(pair, results, outs):
            ref[i] = values
            sent.append(copies.start(ref.at[i], hbm.at[i]))
    sets = []
    for arr, ref in enumerate(results):
        edges = [ref[band, :96].reshape(12, 8, 512) for band in range(bands)]
        for level in range(2):
            first = WIN_LAT * level
            rows = [edge[first : first + WIN_LAT] for edge in edges[:-1]]
            sets.append(jnp.concatenate(rows + [edges[-1][first : first + 3]], axis=0))
        a, b, c = windows_to_band(ref[bands].astype(F32), ref[bands - 1].astype(F32))
        planes = jnp.concatenate([a, b, c], axis=1).astype(BF16)
        for level in range(2):
            lat_out[arr, level] = planes[WIN_LAT * level + 3 : WIN_LAT * level + 6]
    for k, packed in enumerate(pack_edges(sets)):
        lon_out[k] = packed
    for copy in sent:
        copy.wait()


def forward_kernel(lat_ref, lon_ref, out_ref):
    rows = lon_ref.shape[1]
    sets = [lat_ref[k // 2, k % 2, :, :8] for k in range(4)]
    for k, packed in enumerate(pack_edges(sets)):
        out_ref[k, :rows] = lon_ref[k]
        out_ref[k, rows:] = packed


def merge_kernel(*refs):
    ins, lat_ref, outs, (left_ref, *refs) = refs[:4], refs[4], refs[5:7], refs[7:]
    held, results, sems = refs[:4], refs[4:6], refs[6]
    copies = Copies(sems)
    got = [copies.start(ins[k], held[k]) for k in range(4)]
    rows = results[0].shape[1]
    bands = rows // WIN_LAT
    sent = []
    for arr, dest in enumerate(results):
        first, second = held[2 * arr], held[2 * arr + 1]
        for level in range(2):
            dest[level, :3] = lat_ref[arr, level]
        got[2 * arr].wait()
        got[2 * arr + 1].wait()
        for band in range(bands):
            w0 = first[band] if band < bands - 1 else second[bands]
            a, b, c = windows_to_band(w0.astype(F32), second[band].astype(F32))
            planes = jnp.concatenate([a, b, c], axis=1).astype(BF16)
            start = 3 + band * WIN_LAT
            size = min(WIN_LAT, rows - start)
            for level in range(2):
                own = slice(level * WIN_LAT, level * WIN_LAT + size)
                dest[level, start : start + size] = planes[own]
        sent.append(copies.start(dest, outs[arr]))
        left_ref[arr] = dest[:, :, :16]
    for copy in sent:
        copy.wait()


def patch_kernel(left_ref, lon_ref, out_hbm, grad_hbm, out_new, grad_new, patch_ref, sems):
    copies = Copies(sems)
    rows = left_ref.shape[2]
    sent = []
    for arr, hbm in enumerate((out_new, grad_new)):
        for level in range(2):
            for start, place, size in ((0, 3, rows - 3), (rows - 3, 0, 3)):
                edge = edge_rows(lon_ref, arr, level, start, size)
                tile = left_ref[arr, level, place : place + size].astype(F32)
                left = jnp.where(sublane(edge.shape) < 6, edge, tile[:, :8])
                tile = jnp.concatenate([left, tile[:, 8:]], axis=1).astype(BF16)
                patch_ref[arr, level, place : place + size] = tile
        sent.append(copies.start(patch_ref.at[arr], hbm.at[:, :, :16]))
    for copy in sent:
        copy.wait()


def pair_kernel(mine_ref, other_ref, out_ref):
    out_ref[...] = (mine_ref[...].astype(F32) + other_ref[...].astype(F32)).astype(BF16)


def halve_kernel(where_ref, mine_ref, other_ref, *refs):
    kept, sent = refs[:2], refs[2:]
    half = kept[0].shape[-1]
    x, y = where_ref[3], where_ref[4]

    def terms(chip, columns):
        return mine_ref[chip, :, columns].astype(F32) + other_ref[chip, :, columns].astype(F32)

    for k in range(2):
        first, second = slice(0, half), slice(half, 2 * half)
        kept[0][k] = terms(2 * k + x, first).astype(BF16)
        sent[0][k] = terms(2 * k + 1 - x, first).astype(BF16)
        kept[1][k] = terms(2 * y + k, second).astype(BF16)
        sent[1][k] = terms(2 * (1 - y) + k, second).astype(BF16)


def quarter_kernel(where_ref, *refs):
    kept, got, keep, send = refs[:2], refs[2:4], refs[4:6], refs[6:8]
    x, y = where_ref[3], where_ref[4]
    for arr, bit in ((0, y), (1, x)):
        keep[arr][...] = kept[arr][bit].astype(F32) + got[arr][bit].astype(F32)
        out = kept[arr][1 - bit].astype(F32) + got[arr][1 - bit].astype(F32)
        send[arr][...] = out.astype(BF16)


def spread(where_ref, total, own_ref, sends, held_ref):
    count, rows = held_ref.shape[0], held_ref.shape[1]
    for i in range(count):
        held_ref[i] = total[rows * i : rows * i + rows]
    me = where_ref[2]
    own_ref[...] = held_ref[me]
    for k, ref in enumerate(sends):
        ref[...] = held_ref[lax.rem(me + 1 + k, count)].astype(BF16)


def pieces_kernel(where_ref, pieces_ref, own_ref, *refs):
    total = pieces_ref[0].astype(F32)
    for i in range(1, pieces_ref.shape[0]):
        total = total + pieces_ref[i].astype(F32)
    spread(where_ref, total, own_ref, refs[:-1], refs[-1])


def halves_kernel(where_ref, *refs):
    keep, got, (own_ref, *refs) = refs[:2], refs[2:4], refs[4:]
    sums = [keep[arr][...] + got[arr][...].astype(F32) for arr in range(2)]
    spread(where_ref, jnp.concatenate(sums, axis=1), own_ref, refs[:-1], refs[-1])


def owner_kernel(own_ref, *refs):
    total = own_ref[...]
    for ref in refs[:-2]:
        total = total + ref[...].astype(F32)
    qkv_ref, out_ref = refs[-2:]
    width = qkv_ref.shape[-1]
    qkv_ref[...] = total[:, :width]
    out_ref[...] = total[:, width:]


def shapes(*items):
    return [jax.ShapeDtypeStruct(shape, dtype) for shape, dtype in items]


VMEM = pl.BlockSpec(memory_space=pltpu.VMEM)
SMEM = pl.BlockSpec(memory_space=pltpu.SMEM)
HBM = pl.BlockSpec(memory_space=pltpu.HBM)


def call(kernel, args, out_shape, micros, scratch=(), scalars=0, ins=VMEM, outs=VMEM, aliases=None):
    moved = sum(a.size * a.dtype.itemsize for a in args)
    out_specs = list(outs) if isinstance(outs, (list, tuple)) else [outs] * len(out_shape)
    out_shape = [
        pltpu.HBM(item.shape, item.dtype) if spec is HBM else item
        for item, spec in zip(out_shape, out_specs)
    ]
    in_specs = list(ins) if isinstance(ins, (list, tuple)) else [ins] * (len(args) - scalars)
    args = [
        pltpu.with_memory_space_constraint(arg, pltpu.HBM) if spec is HBM else arg
        for arg, spec in zip(args, [SMEM] * scalars + in_specs)
    ]
    return pl.pallas_call(
        kernel,
        out_shape=out_shape,
        in_specs=[SMEM] * scalars + in_specs,
        out_specs=out_specs,
        scratch_shapes=list(scratch),
        input_output_aliases=aliases or {},
        compiler_params=pltpu.CompilerParams(vmem_limit_bytes=VMEM_LIMIT),
        cost_estimate=pl.CostEstimate(
            flops=int(micros * 10**9), bytes_accessed=moved, transcendentals=0
        ),
    )(*args)


def room(items):
    return [pltpu.VMEM(item.shape, item.dtype) for item in items]


def shift(x, lon_by, lat_by):
    lons, lats = lax.axis_size("lon"), lax.axis_size("lat")
    pairs = []
    for i in range(lons):
        for j in range(lats):
            to = (i + lon_by) % lons * lats + (j + lat_by) % lats
            pairs.append((i * lats + j, to))
    return lax.ppermute(x, ("lon", "lat"), pairs)


def partner(x, axis, flip):
    return lax.ppermute(x, axis, [(i, i ^ flip) for i in range(lax.axis_size(axis))])


def exchange(pieces, axis, groups=None):
    return lax.all_to_all(pieces, axis, 0, 0, axis_index_groups=groups, tiled=True)


def shards(fields, cotangent, qkv_weight, out_weight):
    levels, lat_cells, lon_cells, width = fields.shape
    lons, lats = lax.axis_size("lon"), lax.axis_size("lat")
    sems = pltpu.SemaphoreType.DMA
    halos = shapes(
        ((2, 2, 3, lon_cells, width), BF16),
        ((3, lat_cells - 3, 8, width), BF16),
        ((2, 2, 3, 8, width), BF16),
    )
    lat_edge, lon_edge, corner = call(
        pack_kernel,
        (fields, cotangent),
        halos,
        1,
        scratch=[pltpu.VMEM((2, 2, lat_cells - 3, 16, width), BF16), sems((4,))],
        ins=HBM,
    )
    lon_edge = shift(lon_edge, -1, 0)
    lat_edge = shift(lat_edge, 0, -1)
    corner = shift(corner, -1, -1)
    row = lax.axis_index("lat")
    lon = lax.axis_index("lon")
    position = jnp.stack(
        [(row == lats - 1).astype(jnp.int32), lon % 2, row, lon // 2 % 2, lon // 4 % 2]
    )
    bands = lat_cells // WIN_LAT

    def windows(count, cols=width):
        return jax.ShapeDtypeStruct((count, TOKENS, cols), BF16)

    def whole(*shape):
        return jax.ShapeDtypeStruct(shape, BF16)

    count = bands - 1
    state = [windows(count)] * 3 + [windows(count, 3 * width)] + [windows(count)] * 2
    band = whole(count, levels, WIN_LAT, lon_cells, width)
    *in_terms, out_in, grad_in = call(
        inner_kernel,
        (fields, cotangent, qkv_weight, out_weight),
        state,
        11,
        scratch=room((band, band, windows(count)))
        + room((windows(count, 2 * width), whole(width, width)))
        + [sems((4 * count + 4,))]
        + room(state),
        ins=[HBM, HBM, VMEM, VMEM],
        outs=HBM,
    )
    count = bands + 1
    rows = width // lons
    terms = whole(lons // 2, rows, 4 * width)
    weights = (qkv_weight, out_weight)
    *outer, mine, send = call(
        outer_kernel,
        (position, fields, cotangent, lat_edge, lon_edge, corner, *weights, *in_terms),
        [windows(count)] * 3 + [windows(count, 3 * width), terms, terms],
        20,
        scratch=room((fields, cotangent, *in_terms, out_weight))
        + room((windows(count), windows(count, 2 * width), whole(width, width)))
        + [pltpu.VMEM((TOKENS, 256), F32), pltpu.VMEM((width, 4 * width), BF16)]
        + [sems((2 * bands + 5,))],
        scalars=1,
        ins=[HBM] * 2 + [VMEM] * 4 + [HBM] * 5,
    )
    received = partner(send, "lon", 1)
    square = lons // 2 == 4
    chips = [[2 * i + core for i in range(lons // 2)] for core in range(2)]
    if square:
        half = whole(2, rows, 2 * width)
        *kept, first, second = call(
            halve_kernel, (position, mine, received), [half] * 4, 1, scalars=1
        )
        first, second, outer[0] = lax.optimization_barrier((first, second, outer[0]))
        parts = [partner(first, "lon", 2), partner(second, "lon", 4)]
    else:
        (total,) = call(pair_kernel, (mine, received), [terms], 1)
        total, outer[0] = lax.optimization_barrier((total, outer[0]))
        parts = [exchange(total, "lon", chips)]
    results = [windows(count)] * 2
    out_out, grad_out, lat_out, lon_out = call(
        outer_back_kernel,
        (*outer, *weights),
        results + halos[:2],
        5,
        scratch=room(results) + [sems((2 * count,))],
        outs=[HBM] * 2 + [VMEM] * 2,
    )
    parts, lon_out = lax.optimization_barrier((parts, lon_out))
    lat_out = shift(lat_out, 0, 1)
    (lon_out,) = call(forward_kernel, (lat_out, lon_out), [whole(3, lat_cells, 8, width)], 1)
    own = width // (lons * lats)
    shares = shapes(((own, 4 * width), F32), *[((own, 4 * width), BF16)] * (lats - 1))
    if square:
        quarter = (rows, 2 * width)
        *kept, first, second = call(
            quarter_kernel,
            (position, *kept, *parts),
            shapes((quarter, F32), (quarter, F32), (quarter, BF16), (quarter, BF16)),
            1,
            scalars=1,
        )
        parts = [partner(first, "lon", 4), partner(second, "lon", 2)]
        parts, _ = lax.optimization_barrier((parts, lon_out))
        parts = (*kept, *parts)
    lon_out = shift(lon_out, 1, 0)
    own, *sends = call(
        halves_kernel if square else pieces_kernel,
        (position, *parts),
        shares,
        1,
        scratch=[pltpu.VMEM((lats, own, 4 * width), F32)],
        scalars=1,
    )
    sends, out_in, grad_in = lax.optimization_barrier((sends, out_in, grad_in))
    got = [shift(piece, 0, 1 + k) for k, piece in enumerate(sends)]
    args = (out_in, out_out, grad_in, grad_out)
    results = shapes((fields.shape, BF16), (fields.shape, BF16))
    left = whole(2, levels, lat_cells, 16, width)
    *results, left = call(
        merge_kernel,
        args + (lat_out,),
        results + [left],
        4,
        scratch=room(args) + room(results) + [sems((6,))],
        ins=[HBM] * 4 + [VMEM],
        outs=[HBM] * 2 + [VMEM],
    )
    output_field, field_grad = call(
        patch_kernel,
        (left, lon_out, *results),
        results,
        2,
        scratch=room((left,)) + [sems((2,))],
        ins=[VMEM] * 2 + [HBM] * 2,
        outs=HBM,
        aliases={2: 0, 3: 1},
    )
    got, output_field, field_grad = lax.optimization_barrier((got, output_field, field_grad))
    qkv_grad, out_grad = call(
        owner_kernel,
        (own, *got),
        shapes(((own.shape[0], 3 * width), F32), ((own.shape[0], width), F32)),
        1,
    )
    return output_field, field_grad, qkv_grad, out_grad


def solution(mesh):
    placed = (P(None, "lat", "lon", None), P(None, "lat", "lon", None), P(), P())
    return jax.shard_map(
        shards,
        mesh=mesh,
        in_specs=placed,
        out_specs=(
            P(None, "lat", "lon", None),
            P(None, "lat", "lon", None),
            P(("lon", "lat"), None),
            P(("lon", "lat"), None),
        ),
        check_vma=False,
    )
```
